32 devices in a mesh: groups: 2 (over y), gx: 16 (over z, x, core).
Axes of the slice: x: 2, y: 2, z: 4, core: 2. Of those that a mesh axis runs over, the one named last changes fastest.
Arguments:
- states: float32 [2, 4, 128, 512], P(None, 'groups', 'gx'), parts along dimension 1, may hold values from -5 to 5
- pre_acts: bfloat16 [2, 3, 256, 48, 512], P(None, None, ('groups', 'gx')), parts along dimension 2, may hold values from -6 to 6
- cotangent: float32 [4, 128, 512], P('groups', 'gx'), parts along dimension 0, may hold values from -12 to 12
- weight_in: bfloat16 [9, 48, 2], replicated, may hold values from -1.5 to 1.5
- weight_second: bfloat16 [9, 48, 48], replicated, may hold values from -0.3125 to 0.3125
- weight_third: bfloat16 [9, 48, 48], replicated, may hold values from -0.3125 to 0.3125
- weight_out: bfloat16 [9, 2, 48], replicated, may hold values from -0.3125 to 0.3125
Outputs:
- state_adjoint: float32 [4, 128, 512], P('groups', 'gx'), parts along dimension 0
- grad_in: float32 [18, 48, 2], P('groups'), parts along dimension 0
- grad_second: float32 [18, 48, 48], P('groups'), parts along dimension 0
- grad_third: float32 [18, 48, 48], P('groups'), parts along dimension 0
- grad_out: float32 [18, 2, 48], P('groups'), parts along dimension 0
The draws below stay inside these ranges and needn't reach their ends.
There are 2 independent parts, one for each index of `groups`. The reference program is written for one: setup_inputs(seed, part) draws one part's arguments, and reference() takes and returns one part's arrays. A program takes and returns all parts, laid end to end along the dimension named above; an argument that names none is the same for every part. Nothing has to cross between parts.
All inputs are finite; a program needn't handle non-finite values.
Results may differ from the reference program's by a relative error of at most 0.0065.
Values may be sent and summed in bfloat16 or wider, within the bound.
A program may use at most 64 MiB of HBM per device.

```python
import math
import jax
import jax.numpy as jnp

CH = 48
NY = 512
NX = 128


def draw_cotangent(key, part):
    ramp = 1.0 + 2.0 * jnp.arange(NX, dtype=jnp.float32) / (NX - 1)
    base = jnp.clip(jax.random.normal(key, (2, NX, NY), jnp.float32), -4.0, 4.0)
    return base * ramp[None, :, None]


def block_scale(key, extent, cuts, smallest, top_value):
    factor_of = 1.0
    for dim, parts in cuts:
        heights = jax.random.uniform(jax.random.fold_in(jax.random.fold_in(key, 6), dim), (parts,), jnp.float32, smallest / len(cuts), top_value / len(cuts))
        factor_of = factor_of * jnp.repeat(jnp.exp(heights), extent[dim] // parts).reshape((-1,) + (1,) * (len(extent) - 1 - dim))
    return factor_of


def gaussian(own_key, shape, deviation, most, split=(), held_as=jnp.bfloat16):
    values = deviation * jax.random.normal(own_key, shape, jnp.float32)
    if split:
        values = values * block_scale(own_key, shape, split, -0.22, 0.18)
    return jnp.clip(values, -most, most).astype(held_as)


def setup_inputs(seed: int = 0, part: int = 0) -> dict:
    splits = jax.random.split(jax.random.key(seed), 8)
    part_keys = jax.random.split(jax.random.fold_in(splits[7], part), 8)
    states = gaussian(part_keys[0], (2, 2, NX, NY), 1.0, 5.0, ((2, 16),), jnp.float32)
    pre_acts = gaussian(part_keys[1], (2, 3, NX, CH, NY), 1.0, 6.0, ((2, 16),))
    cotangent = draw_cotangent(jax.random.fold_in(jax.random.fold_in(splits[7], part), 71), part)
    weight_in = gaussian(splits[3], (9, CH, 2), 18 ** -0.5, 1.5)
    weight_second = gaussian(splits[4], (9, CH, CH), (9 * CH) ** -0.5, 0.3125)
    weight_third = gaussian(splits[5], (9, CH, CH), (9 * CH) ** -0.5, 0.3125)
    weight_out = gaussian(splits[6], (9, 2, CH), (9 * CH) ** -0.5, 0.3125)
    return {"states": states, "pre_acts": pre_acts, "cotangent": cotangent, "weight_in": weight_in, "weight_second": weight_second, "weight_third": weight_third, "weight_out": weight_out}


step_factor = 0.25
viscosity = 0.4

def pad_rows(values, rim_width):
    return jnp.concatenate([values[:, -rim_width:], values, values[:, :rim_width]], axis=1)

def pad_lead(values, rim_width):
    return jnp.concatenate([values[-rim_width:], values, values[:rim_width]], axis=0)

def half_valid(state_ext):
    row_count = state_ext.shape[1] - 2
    row_speed = state_ext[0]
    col_speed = state_ext[1][1:row_count + 1]
    face_speed = 0.25 * (row_speed[:-1] + row_speed[1:])
    side_speed = 0.25 * (col_speed + jnp.roll(col_speed, -1, axis=-1))
    outputs = []
    for component in range(2):
        values = state_ext[component]
        middle = values[1:row_count + 1]
        row_flux = face_speed * (values[:-1] + values[1:])
        col_flux = side_speed * (middle + jnp.roll(middle, -1, axis=-1))
        divergence = row_flux[1:] - row_flux[:-1] + (col_flux - jnp.roll(col_flux, 1, axis=-1))
        laplacian = values[2:] + values[:-2] + jnp.roll(middle, -1, axis=-1) + jnp.roll(middle, 1, axis=-1) - 4.0 * middle
        outputs.append(middle + step_factor * (viscosity * laplacian - divergence))
    return jnp.stack(outputs)

def relu_value(preact):
    return jnp.maximum(preact.astype(jnp.float32), jnp.float32(0.0))

def relu_slope(preact):
    return jnp.where(preact > 0, jnp.float32(1.0), jnp.float32(0.0))

def col_shifts(values):
    return [jnp.roll(values, 1, axis=-1), values, jnp.roll(values, -1, axis=-1)]

def weight_terms(gradient, source_ext):
    row_count = gradient.shape[0]
    shifted = col_shifts(source_ext)
    grad_wide = gradient.astype(jnp.float32)
    products = []
    for row_tap in range(3):
        for col_tap in range(3):
            section = shifted[col_tap][row_tap:row_tap + row_count].astype(jnp.float32)
            products.append(jnp.einsum('roy,rky->ok', grad_wide, section))
    return jnp.stack(products)

def back_conv(grad_ext, kernel):
    row_count = grad_ext.shape[0] - 2
    shifted = col_shifts(grad_ext)
    summed = None
    for row_tap in range(3):
        for col_tap in range(3):
            section = shifted[2 - col_tap][2 - row_tap:2 - row_tap + row_count].astype(jnp.float32)
            product = jnp.einsum('ok,roy->rky', kernel[3 * row_tap + col_tap].astype(jnp.float32), section)
            summed = product if summed is None else summed + product
    return summed

def backward_step(state, preacts, adjoint, kernels):
    half_value, pullback = jax.vjp(lambda values: half_valid(pad_rows(values, 1)), state)
    source_first = pad_lead(jnp.swapaxes(half_value, 0, 1).astype(jnp.bfloat16), 1)
    gradient = jnp.swapaxes(adjoint, 0, 1).astype(jnp.bfloat16)
    results = [None, None, None, None]
    backward = None
    for layer_index in (3, 2, 1, 0):
        if layer_index > 0:
            source = pad_lead(relu_value(preacts[layer_index - 1]).astype(jnp.bfloat16), 1)
        else:
            source = source_first
        results[layer_index] = weight_terms(gradient, source)
        backward = back_conv(pad_lead(gradient, 1), kernels[layer_index])
        if layer_index > 0:
            gradient = (backward * relu_slope(preacts[layer_index - 1])).astype(jnp.bfloat16)
    combined = adjoint + jnp.swapaxes(backward, 0, 1)
    return (pullback(combined)[0], results)

def reference(states, pre_acts, cotangent, weight_in, weight_second, weight_third, weight_out):
    kernels = (weight_in, weight_second, weight_third, weight_out)
    grad_totals = [jnp.zeros(kernel.shape, jnp.float32) for kernel in kernels]
    adjoint = cotangent
    for step_index in (1, 0):
        adjoint, results = backward_step(states[step_index], pre_acts[step_index], adjoint, kernels)
        grad_totals = [grad_totals[number] + results[number] for number in range(4)]
    factor = 1.0 / math.sqrt(NX * NY)
    return (adjoint, grad_totals[0] * factor, grad_totals[1] * factor, grad_totals[2] * factor, grad_totals[3] * factor)
```

```python
import functools
import math

import jax
import jax.numpy as jnp
from jax import lax
from jax.experimental import pallas as pl
from jax.experimental.pallas import tpu as pltpu
from jax.sharding import PartitionSpec as P

step_factor = 0.25
viscosity = 0.4
lane_pad = 8
MESH = pl.DeviceIdType.MESH
IN_KERNEL_SUM = True


def roll_cols(values, amount):
    return pltpu.roll(values, amount % values.shape[-1], values.ndim - 1)


def roll_rows(values, amount):
    return pltpu.roll(values, amount % values.shape[-2], values.ndim - 2)


def east(values):
    return roll_cols(values, -1)


def west(values):
    return roll_cols(values, 1)


def south(values):
    return roll_rows(values, -1)


def north(values):
    return roll_rows(values, 1)


def half_step(row_speed, col_speed):
    face = 0.25 * (row_speed + south(row_speed))
    side = 0.25 * (col_speed + east(col_speed))
    outputs = []
    for values in (row_speed, col_speed):
        below, right = south(values), east(values)
        row_flux = face * (values + below)
        col_flux = side * (values + right)
        divergence = row_flux - north(row_flux) + (col_flux - west(col_flux))
        laplacian = below + north(values) + right + west(values) - 4.0 * values
        outputs.append(values + step_factor * (viscosity * laplacian - divergence))
    return outputs


def half_step_adjoint(row_speed, col_speed, grads):
    face = 0.25 * (row_speed + south(row_speed))
    side = 0.25 * (col_speed + east(col_speed))
    outputs = []
    face_grad = None
    side_grad = None
    for values, grad in zip((row_speed, col_speed), grads):
        below, right = south(grad), east(grad)
        row_part = step_factor * (below - grad)
        col_part = step_factor * (right - grad)
        laplacian = below + north(grad) + right + west(grad) - 4.0 * grad
        row_back = row_part * face
        col_back = col_part * side
        outputs.append(
            grad
            + (step_factor * viscosity) * laplacian
            + (row_back + north(row_back))
            + (col_back + west(col_back))
        )
        face_term = row_part * (values + south(values))
        side_term = col_part * (values + east(values))
        face_grad = face_term if face_grad is None else face_grad + face_term
        side_grad = side_term if side_grad is None else side_grad + side_term
    return [
        outputs[0] + 0.25 * (face_grad + north(face_grad)),
        outputs[1] + 0.25 * (side_grad + west(side_grad)),
    ]


def matmul(left, right):
    return lax.dot_general(left, right, (((1,), (0,)), ((), ())), preferred_element_type=jnp.float32)


def matmul_nt(left, right):
    return lax.dot_general(left, right, (((1,), (1,)), ((), ())), preferred_element_type=jnp.float32)


def kernel(
    count,
    pieces,
    scale,
    states,
    acts,
    cot,
    w_in,
    w_second,
    w_third,
    w_out,
    adj_out,
    sum_out,
    hal_u,
    hal_g,
    hal_a,
    hal_d,
    snd_d,
    grid_g,
    stage,
    wide,
    source,
    ghs,
    part,
    gathered,
    w2t,
    w3t,
    sem_u,
    sem_g,
    sem_a,
    sem_d,
    sem_rs,
    sem_ag,
):
    rows, cols = cot.shape[1], cot.shape[2]
    ch = acts.shape[3]
    me = lax.axis_index("gx")
    prev = lax.rem(me + count - 1, count)
    nxt = lax.rem(me + 1, count)

    barrier = pltpu.get_barrier_semaphore()
    if IN_KERNEL_SUM:

        def greet(k, carry):
            peer = lax.rem(me + k, count)
            pl.semaphore_signal(barrier, inc=1, device_id={"gx": peer}, device_id_type=MESH)
            return carry

        lax.fori_loop(1, count, greet, 0)
        pl.semaphore_wait(barrier, count - 1)
    else:
        for peer in (prev, nxt):
            pl.semaphore_signal(barrier, inc=1, device_id={"gx": peer}, device_id_type=MESH)
        pl.semaphore_wait(barrier, 2)

    def exchange(up_src, down_src, dst, sems):
        copies = []
        for src, side, peer in ((up_src, 1, prev), (down_src, 0, nxt)):
            copy = pltpu.make_async_remote_copy(
                src_ref=src,
                dst_ref=dst.at[side],
                send_sem=sems.at[0, side],
                recv_sem=sems.at[1, side],
                device_id={"gx": peer},
                device_id_type=MESH,
            )
            copy.start()
            copies.append(copy)
        return copies

    def arrived(copies):
        for copy in copies:
            copy.wait_recv()

    started = []
    cot_moves = exchange(cot, cot, hal_g.at[0], sem_g.at[0])
    act_moves = [None, None]
    act_moves[1] = exchange(acts.at[1, 2, 0], acts.at[1, 2, rows - 1], hal_a.at[1], sem_a.at[1])
    state_moves = exchange(states, states, hal_u, sem_u)
    act_moves[0] = exchange(acts.at[0, 2, 0], acts.at[0, 2, rows - 1], hal_a.at[0], sem_a.at[0])
    started += cot_moves + act_moves[0] + act_moves[1] + state_moves

    stage[...] = jnp.zeros_like(stage)
    source[...] = jnp.zeros_like(source)
    w2t[...] = jnp.transpose(w_second[...].astype(jnp.float32)).astype(jnp.bfloat16)
    w3t[...] = jnp.transpose(w_third[...].astype(jnp.float32)).astype(jnp.bfloat16)

    row_block = 3 * ch

    def put_row(buffer, row, values):
        place = (rows - row) * row_block
        wide[buffer, place : place + ch, :] = roll_cols(values, -1).astype(jnp.bfloat16)
        wide[buffer, place + ch : place + 2 * ch, :] = values.astype(jnp.bfloat16)
        wide[buffer, place + 2 * ch : place + 3 * ch, :] = roll_cols(values, 1).astype(jnp.bfloat16)

    def neighbourhood(buffer, row):
        place = (rows - 1 - row) * row_block
        return wide[buffer, place : place + 3 * row_block, :]

    def relu(values):
        return jnp.maximum(values.astype(jnp.float32), 0.0).astype(jnp.bfloat16)

    def masked(values, preact):
        kept = jnp.where(preact.astype(jnp.float32) > 0.0, values, 0.0)
        return kept.astype(jnp.bfloat16).astype(jnp.float32)

    def total(place, value, first):
        if first:
            part[place] = value
        else:
            part[place] = part[place] + value

    exchange_no = 0
    for step in (1, 0):
        first = step == 1
        if first:
            arrived(cot_moves)
            for comp in range(2):
                grid_g[comp, 0:rows, :] = hal_g[0, 0, comp]
                grid_g[comp, rows : 2 * rows, :] = cot[comp]
                grid_g[comp, 2 * rows : 3 * rows, :] = hal_g[0, 1, comp]
        for comp in range(2):
            values = grid_g[comp]
            for shift in range(3):
                moved = roll_cols(values, shift - 1) if shift != 1 else values
                for row in range(-2, rows + 2):
                    place = (rows + 1 - row) * 24 + shift * 8 + comp
                    stage[place : place + 1, :] = moved[row + rows : row + rows + 1, :]

        def stage_rows(row):
            place = (rows - row) * 24
            return stage[place : place + 72, :].astype(jnp.bfloat16)

        arrived(act_moves[step])
        for row in range(-1, rows + 1):
            if row < 0:
                preact = hal_a[step, 0]
            elif row >= rows:
                preact = hal_a[step, 1]
            else:
                preact = acts[step, 2, row]
            put_row(0, row, masked(matmul(w_out[...], stage_rows(row)), preact))

        def out_terms():
            acc = None
            for row in range(rows):
                term = matmul_nt(relu(acts[step, 2, row]), stage_rows(row))
                acc = term if acc is None else acc + term
            half = ch // 2
            total((pl.ds(2 * ch + 8, half), pl.ds(0, 72)), acc[:half], first)
            total((pl.ds(2 * ch + 8, half), pl.ds(128, 72)), acc[half:], first)

        def hidden_terms(layer, buffer):
            acc = None
            for row in range(rows):
                term = matmul_nt(relu(acts[step, layer, row]), neighbourhood(buffer, row))
                acc = term if acc is None else acc + term
            total((pl.ds(layer * ch, ch), pl.ds(0, 3 * row_block)), acc, first)

        for layer, kernel_t, buffer in ((1, w3t, 0), (0, w2t, 1)):
            target = 1 - buffer
            for row in (0, rows - 1):
                values = masked(matmul(kernel_t[...], neighbourhood(buffer, row)), acts[step, layer, row])
                snd_d[exchange_no, 0 if row == 0 else 1] = values.astype(jnp.bfloat16)
                put_row(target, row, values)
            moves = exchange(
                snd_d.at[exchange_no, 0], snd_d.at[exchange_no, 1], hal_d.at[exchange_no], sem_d.at[exchange_no]
            )
            started += moves
            for row in range(1, rows - 1):
                values = masked(matmul(kernel_t[...], neighbourhood(buffer, row)), acts[step, layer, row])
                put_row(target, row, values)
            if layer == 1:
                out_terms()
            hidden_terms(layer, buffer)
            if layer == 0:
                if first:
                    arrived(state_moves)
                speeds = [
                    jnp.concatenate(
                        [hal_u[0, step, comp], states[step, comp], hal_u[1, step, comp]], axis=0
                    )
                    for comp in range(2)
                ]
                halves = half_step(*speeds)
                for comp in range(2):
                    for row in range(rows):
                        place = row * 16 + comp
                        source[place : place + 1, :] = halves[comp][row + rows : row + rows + 1, :]
            arrived(moves)
            put_row(target, -1, hal_d[exchange_no, 0].astype(jnp.float32))
            put_row(target, rows, hal_d[exchange_no, 1].astype(jnp.float32))
            exchange_no += 1

        for row in range(rows):
            back = matmul(w_in[...], neighbourhood(0, row))
            for comp in range(2):
                ghs[1 - step, comp, row : row + 1, :] = (
                    back[comp : comp + 1] + grid_g[comp, rows + row : rows + row + 1, :]
                )
        slot = 1 + (1 - step)
        moves = exchange(ghs.at[1 - step], ghs.at[1 - step], hal_g.at[slot], sem_g.at[slot])
        started += moves
        acc = None
        for row in range(rows):
            term = matmul_nt(
                source[row * 16 : row * 16 + 16, :].astype(jnp.bfloat16), neighbourhood(0, row)
            )
            acc = term if acc is None else acc + term
        total((pl.ds(2 * ch, 8), pl.ds(0, 3 * row_block)), acc[:8], first)

        if step == 0 and IN_KERNEL_SUM:
            reducing = functools.partial(scatter_sum, count, pieces, me, part, gathered, sem_rs)
            reducing()

        arrived(moves)
        grads = [
            jnp.concatenate([hal_g[slot, 0, comp], ghs[1 - step, comp], hal_g[slot, 1, comp]], axis=0)
            for comp in range(2)
        ]
        fresh = half_step_adjoint(speeds[0], speeds[1], grads)
        for comp in range(2):
            if step == 0:
                adj_out[comp] = fresh[comp][rows : 2 * rows]
            else:
                grid_g[comp] = fresh[comp]

    if IN_KERNEL_SUM:
        share_sum(count, pieces, scale, me, part, gathered, sum_out, sem_rs, sem_ag)
    else:
        sum_out[...] = part[...]
    for copy in started:
        copy.wait_send()


def scatter_sum(count, pieces, me, part, gathered, sem_rs):
    height = part.shape[0] // pieces

    def send(k, carry):
        peer = lax.rem(me + k, count)

        def go():
            pltpu.make_async_remote_copy(
                src_ref=part.at[pl.ds(pl.multiple_of(peer * height, height), height)],
                dst_ref=gathered.at[me],
                send_sem=sem_rs.at[0, k],
                recv_sem=sem_rs.at[1, me],
                device_id={"gx": peer},
                device_id_type=MESH,
            ).start()

        if pieces == count:
            go()
        else:
            pl.when(peer < pieces)(go)
        return carry

    lax.fori_loop(1, count, send, 0)


def share_sum(count, pieces, scale, me, part, gathered, sum_out, sem_rs, sem_ag):
    height = part.shape[0] // pieces

    def reduce_and_send():
        mine = pl.ds(pl.multiple_of(me * height, height), height)

        def add(k, acc):
            peer = lax.rem(me + k, count)
            pltpu.make_async_copy(gathered.at[peer], gathered.at[peer], sem_rs.at[1, peer]).wait()
            return acc + gathered[peer]

        sum_out[mine, :] = lax.fori_loop(1, count, add, part[mine, :]) * scale

        def send(k, carry):
            peer = lax.rem(me + k, count)
            pltpu.make_async_remote_copy(
                src_ref=sum_out.at[mine],
                dst_ref=sum_out.at[mine],
                send_sem=sem_ag.at[0, k],
                recv_sem=sem_ag.at[1, me],
                device_id={"gx": peer},
                device_id_type=MESH,
            ).start()
            return carry

        lax.fori_loop(1, count, send, 0)

        def sent(k, carry):
            pltpu.make_async_copy(gathered.at[0], gathered.at[0], sem_ag.at[0, k]).wait()
            return carry

        lax.fori_loop(1, count, sent, 0)

    if pieces == count:
        reduce_and_send()
    else:
        pl.when(me < pieces)(reduce_and_send)

    def finish(k, carry):
        peer = lax.rem(me + k, count)

        def go():
            pltpu.make_async_copy(gathered.at[0], gathered.at[0], sem_rs.at[0, k]).wait()
            spot = sum_out.at[pl.ds(pl.multiple_of(peer * height, height), height)]
            pltpu.make_async_copy(spot, spot, sem_ag.at[1, peer]).wait()

        if pieces == count:
            go()
        else:
            pl.when(peer < pieces)(go)
        return carry

    lax.fori_loop(1, count, finish, 0)


def on_device(states, pre_acts, cotangent, weight_in, weight_second, weight_third, weight_out):
    count = lax.axis_size("gx")
    rows, cols = cotangent.shape[1], cotangent.shape[2]
    ch = pre_acts.shape[3]
    taps = weight_in.shape[0]
    scale = 1.0 / math.sqrt(rows * count * cols)
    w_in = jnp.pad(jnp.transpose(weight_in.reshape(taps * ch, 2)), ((0, 14), (0, 0)))
    w_out = jnp.transpose(jnp.pad(weight_out, ((0, 0), (0, lane_pad - 2), (0, 0))).reshape(taps * lane_pad, ch))
    total_rows = 2 * ch + 8 + ch // 2
    pieces = total_rows // 8
    while pieces > count or total_rows % pieces:
        pieces //= 2
    tall = taps * ch
    vmem = pl.BlockSpec(memory_space=pltpu.VMEM)
    f32, bf16 = jnp.float32, jnp.bfloat16
    dma = pltpu.SemaphoreType.DMA
    adjoint, sums = pl.pallas_call(
        functools.partial(kernel, count, pieces, scale),
        out_shape=(
            jax.ShapeDtypeStruct(cotangent.shape, f32),
            jax.ShapeDtypeStruct((total_rows, cols), f32),
        ),
        in_specs=[vmem] * 7,
        out_specs=(vmem, vmem),
        scratch_shapes=[
            pltpu.VMEM((2, 2, 2, rows, cols), f32),
            pltpu.VMEM((3, 2, 2, rows, cols), f32),
            pltpu.VMEM((2, 2, ch, cols), bf16),
            pltpu.VMEM((4, 2, ch, cols), bf16),
            pltpu.VMEM((4, 2, ch, cols), bf16),
            pltpu.VMEM((2, 3 * rows, cols), f32),
            pltpu.VMEM(((rows + 4) * 24, cols), f32),
            pltpu.VMEM((2, (rows + 2) * 3 * ch, cols), bf16),
            pltpu.VMEM((rows * 16, cols), f32),
            pltpu.VMEM((2, 2, rows, cols), f32),
            pltpu.VMEM((total_rows, cols), f32),
            pltpu.VMEM((count, total_rows // pieces, cols), f32),
            pltpu.VMEM((ch, tall), bf16),
            pltpu.VMEM((ch, tall), bf16),
            dma((2, 2)),
            dma((3, 2, 2)),
            dma((2, 2, 2)),
            dma((4, 2, 2)),
            dma((2, count)),
            dma((2, count)),
        ],
        compiler_params=pltpu.CompilerParams(
            collective_id=0, has_side_effects=True, vmem_limit_bytes=48 * 1024 * 1024
        ),
    )(
        states,
        pre_acts,
        cotangent,
        w_in,
        weight_second.reshape(tall, ch),
        weight_third.reshape(tall, ch),
        w_out,
    )
    if not IN_KERNEL_SUM:
        sums = lax.psum(sums, "gx") * scale
    grad_second = jnp.transpose(sums[:ch, :tall]).reshape(taps, ch, ch)
    grad_third = jnp.transpose(sums[ch : 2 * ch, :tall]).reshape(taps, ch, ch)
    grad_in = jnp.transpose(sums[2 * ch : 2 * ch + 2, :tall]).reshape(taps, ch, 2)
    last = sums[2 * ch + 8 :]
    last = jnp.concatenate([last[:, : taps * lane_pad], last[:, 128 : 128 + taps * lane_pad]], axis=0)
    grad_out = jnp.transpose(last).reshape(taps, lane_pad, ch)[:, :2]
    return (adjoint, grad_in, grad_second, grad_third, grad_out)


def solution(mesh):
    return jax.shard_map(
        on_device,
        mesh=mesh,
        in_specs=(
            P(None, "groups", "gx", None),
            P(None, None, ("groups", "gx"), None, None),
            P("groups", "gx", None),
            P(),
            P(),
            P(),
            P(),
        ),
        out_specs=(
            P("groups", "gx", None),
            P("groups", None, None),
            P("groups", None, None),
            P("groups", None, None),
            P("groups", None, None),
        ),
        check_vma=False,
    )
```
